32 devices in a mesh: row: 4 (over x, core), col: 8 (over z, y).
Axes of the slice: x: 2, y: 2, z: 4, core: 2. Of those that a mesh axis runs over, the one named last changes fastest.
Arguments:
- hamiltonian: float32 [4096, 1024], P('row', 'col'), may hold values from -0.09375 to 0.09375
- pattern: int32 [128, 32], P('row', 'col'), may hold values 0 or 1
- onsite: float32 [4096], P('row'), may hold values from -1 to 1
- members: int32 [32, 32], replicated, may hold values from 0 to 31, as said below
- orders: int32 [32], replicated, may hold values from 16 to 32, as said below
- intersection_inv: bfloat16 [4096, 3, 1024], P(('row', 'col')), may hold values from -6 to 6
Outputs:
- density: float32 [4096, 3, 1024], P(('row', 'col'))
The draws below stay inside these ranges and needn't reach their ends.
Inputs may be any that keep to these rules, and one draw needn't show every extreme that they name: `members`: each row holds 32 distinct team block indices; the first 4 of row g are (g mod 8) * 4 onward in rising order. `orders`: some group has all 32 members active.
All inputs are finite; a program needn't handle non-finite values. No bound on the sum of `pattern` on one device may be relied on, other than what follows from the above.
Results may differ from the reference program's by a relative error of at most 0.0027.
Values may be sent and summed in bfloat16 or wider, within the bound.
No kernel may reach another device: no remote copies, remote signals or barrier semaphores. Data moves between devices by JAX's collectives and lax.ppermute only.
A program may use at most 256 MiB of HBM per device.

```python
import jax
import jax.numpy as jnp
from jax import lax

BLOCK = 32
OWN_BLOCKS = 4
MEMBERS = 32
TEAMS = 4
SLOTS = 8
TEAM_BLOCKS = 32
TEAM_WIDTH = 1024
GROUPS = 32
ALL_ROWS = 4096


def draw_members(key, part):

    def one_group(group_index):
        slot_index = group_index % SLOTS
        own_blocks = slot_index * OWN_BLOCKS + jnp.arange(OWN_BLOCKS, dtype=jnp.int32)
        shuffled = jax.random.permutation(jax.random.fold_in(key, group_index), TEAM_BLOCKS).astype(jnp.int32)
        owned_flag = (shuffled >= slot_index * OWN_BLOCKS) & (shuffled < slot_index * OWN_BLOCKS + OWN_BLOCKS)
        ranking = owned_flag.astype(jnp.int32) * TEAM_BLOCKS + jnp.arange(TEAM_BLOCKS, dtype=jnp.int32)
        picked = shuffled[jnp.argsort(ranking, stable=True)]
        return jnp.concatenate([own_blocks, picked[:MEMBERS - OWN_BLOCKS]]).astype(jnp.int32)
    return jax.vmap(one_group)(jnp.arange(GROUPS, dtype=jnp.int32))


def draw_orders(key, part):
    counts = jax.random.randint(key, (GROUPS,), MEMBERS // 2, MEMBERS + 1)
    fullest = jax.random.randint(jax.random.fold_in(key, 7), (), 0, GROUPS)
    return jnp.where(jnp.arange(GROUPS) == fullest, MEMBERS, counts).astype(jnp.int32)


def touch_ends(entries, rng, least, high):
    extent = entries.shape
    index_at = [jax.random.randint(jax.random.fold_in(rng, axis), (), 0, extent[axis]) for axis in range(len(extent))]
    entries = entries.at[tuple(index_at)].set(least)
    longest = extent.index(max(extent))
    index_at[longest] = (index_at[longest] + 1) % extent[longest]
    return entries.at[tuple(index_at)].set(high)


def level_of(key, shape, pieces, low, largest):
    level, own = 1.0, jax.random.fold_in(key, 6)
    for dim, parts in pieces:
        heights = jnp.exp(jax.random.uniform(jax.random.fold_in(own, dim), (parts,), jnp.float32, low / len(pieces), largest / len(pieces)))
        level = level * jnp.repeat(heights, shape[dim] // parts).reshape([-1 if axis == dim else 1 for axis in range(len(shape))])
    return level


def noise(key, extent, deviation, reach, shards=(), kind=jnp.bfloat16):
    gain = level_of(key, extent, shards, -0.22, 0.18) if shards else 1.0
    values = jax.random.normal(key, extent, jnp.float32) * deviation * gain
    return jnp.minimum(jnp.maximum(values, -reach), reach).astype(kind)


def setup_inputs(seed: int = 0) -> dict:
    key_of = jax.random.split(jax.random.key(seed), 7)
    return {
        "hamiltonian": noise(key_of[0], (ALL_ROWS, TEAM_WIDTH), (4 * MEMBERS * BLOCK) ** -0.5, 0.09375, ((0, 4), (1, 8)), jnp.float32),
        "pattern": touch_ends((jax.random.randint(key_of[1], (TEAMS * TEAM_BLOCKS, TEAM_BLOCKS), 0, 4) < 3).astype(jnp.int32), jax.random.fold_in(key_of[1], 1), 0, 1),
        "onsite": jnp.clip(jax.random.uniform(key_of[2], (ALL_ROWS,), jnp.float32, -1.0, 1.0) * level_of(key_of[2], (ALL_ROWS,), ((0, 4),), -0.4, 0.0), -1.0, 1.0),
        "members": draw_members(jax.random.fold_in(key_of[6], 71), 0),
        "orders": draw_orders(jax.random.fold_in(key_of[6], 71), 0),
        "intersection_inv": noise(key_of[5], (ALL_ROWS, 3, TEAM_WIDTH), 0.7, 6.0, ((0, 32),)),
    }


def element_rows(blocks):
    offsets = jnp.arange(BLOCK, dtype=jnp.int32)
    return (blocks[..., :, None] * BLOCK + offsets).reshape(blocks.shape[:-1] + (-1,)).astype(jnp.int32)

def sign_columns(submatrix, active_count, own_width):
    squares = jnp.sum(submatrix * submatrix)
    factor = jnp.sqrt(active_count.astype(jnp.float32) * BLOCK / (4.0 * (squares + 1e-06)))
    initial = factor * submatrix
    square = jnp.dot(initial, initial, precision=lax.Precision.HIGHEST, preferred_element_type=jnp.float32)
    first_step = 0.5 * (3.0 * initial - jnp.dot(initial, square, precision=lax.Precision.HIGHEST, preferred_element_type=jnp.float32))
    left_cols = first_step[:, :own_width]
    inner_prod = jnp.dot(first_step, left_cols, precision=lax.Precision.HIGHEST, preferred_element_type=jnp.float32)
    return 0.5 * (3.0 * left_cols - jnp.dot(first_step, inner_prod, precision=lax.Precision.HIGHEST, preferred_element_type=jnp.float32))

def reference(hamiltonian, pattern, onsite, members, orders, intersection_inv):
    own_width = OWN_BLOCKS * BLOCK
    weights = jnp.repeat(jnp.repeat(pattern.astype(jnp.float32), BLOCK, axis=0), BLOCK, axis=1)
    team_ham = (hamiltonian * weights).reshape(TEAMS, TEAM_WIDTH, TEAM_WIDTH)
    team_onsite = onsite.reshape(TEAMS, TEAM_WIDTH)

    def one_group(group_index):
        team_index = group_index // SLOTS
        row_ids = element_rows(members[group_index])
        block_ham = lax.dynamic_index_in_dim(team_ham, team_index, 0, keepdims=False)
        coupling = jnp.take(jnp.take(block_ham, row_ids, axis=0), row_ids, axis=1)
        active = jnp.repeat((jnp.arange(MEMBERS) < orders[group_index]).astype(jnp.float32), BLOCK)
        coupling = coupling * active[:, None] * active[None, :]
        diag_vals = jnp.take(lax.dynamic_index_in_dim(team_onsite, team_index, 0, keepdims=False), row_ids) * active
        submatrix = 0.5 * (coupling + coupling.T) + jnp.diag(diag_vals)
        return sign_columns(submatrix, orders[group_index], own_width).astype(jnp.bfloat16)
    sign_blocks = lax.map(one_group, jnp.arange(GROUPS, dtype=jnp.int32))
    rows_all = element_rows(members)
    team_of = jnp.arange(GROUPS, dtype=jnp.int32) // SLOTS
    slot_of = jnp.arange(GROUPS, dtype=jnp.int32) % SLOTS
    team_sign = jnp.zeros((TEAMS, TEAM_WIDTH, SLOTS, own_width), jnp.bfloat16)
    team_sign = team_sign.at[team_of[:, None], rows_all, slot_of[:, None]].set(sign_blocks)
    team_sign = team_sign.reshape(TEAMS, TEAM_WIDTH, TEAM_WIDTH)
    z_teams = intersection_inv.reshape(TEAMS, TEAM_WIDTH, 3, TEAM_WIDTH)

    def one_team(team_index):
        z_team = lax.dynamic_index_in_dim(z_teams, team_index, 0, keepdims=False)
        results = []
        for side_index in range(3):
            other_team = (team_index + side_index - 1) % TEAMS
            sign_team = lax.dynamic_index_in_dim(team_sign, other_team, 0, keepdims=False)
            results.append(jnp.dot(z_team[:, side_index, :], sign_team, preferred_element_type=jnp.float32))
        return jnp.stack(results, axis=1)
    density = lax.map(one_team, jnp.arange(TEAMS, dtype=jnp.int32))
    return density.reshape(ALL_ROWS, 3, TEAM_WIDTH)
```

```python
import jax
import jax.numpy as jnp
from jax import lax
from jax.experimental import pallas as pl
from jax.experimental.pallas import tpu as pltpu
from jax.sharding import PartitionSpec as P

BLOCK = 32
OWN_BLOCKS = 4
MEMBERS = 32
INNER = 2
F32 = jnp.float32
BF16 = jnp.bfloat16
LAST = (((1,), (1,)), ((), ()))


def pairs(count, outer_shift, inner_shift):
    return [(i, i ^ (outer_shift * INNER + inner_shift)) for i in range(count)]


def gather_col(shard):
    count = lax.axis_size("col")
    parts = {}
    parts[0] = shard
    parts[1] = lax.ppermute(shard, "col", pairs(count, 0, 1))
    for shift in range(1, count // INNER):
        parts[shift * INNER] = lax.ppermute(shard, "col", pairs(count, shift, 0))
    for shift in range(1, count // INNER):
        parts[shift * INNER + 1] = lax.ppermute(parts[shift * INNER], "col", pairs(count, 0, 1))
    return [parts[k] for k in range(count)]


def sign_kernel(count, me_ref, active_ref, mask_col, mask_row, diag_row, *refs):
    shards = refs[:count]
    out_ref, ham = refs[count:]
    width = ham.shape[0]
    own = out_ref.shape[0]
    me = me_ref[0]
    squares = jnp.zeros((1, own), F32)
    rows = lax.broadcasted_iota(jnp.int32, (own, own), 0)
    cols = lax.broadcasted_iota(jnp.int32, (own, own), 1)
    eye = rows == cols
    for k in range(count):
        start = pl.multiple_of((me ^ k) * own, own)
        block = shards[k][...] * mask_col[...] * mask_row[:, pl.ds(start, own)]
        ham[:, pl.ds(start, own)] = block
        wide = block.astype(F32)
        squares += 0.5 * jnp.sum(wide * wide, axis=0, keepdims=True)
    for k in range(count):
        start = k * own
        diag = diag_row[:, start : start + own]
        across = ham[start : start + own, :]
        down = ham[:, start : start + own]
        both = jnp.dot(across, down, preferred_element_type=F32)
        here = ham[start : start + own, start : start + own].astype(F32)
        entries = 0.5 * both + 2.0 * diag * here
        squares += jnp.sum(jnp.where(eye, entries, 0.0), axis=0, keepdims=True)
        squares += diag * diag
    total = jnp.sum(squares, axis=1, keepdims=True)
    active_rows = active_ref[0].astype(F32) * BLOCK
    factor = jnp.sqrt(active_rows / (4.0 * (total + 1e-06)))
    diag_all = diag_row[...]

    def times(panel):
        high = panel.astype(BF16)
        low = (panel - high.astype(F32)).astype(BF16)
        stacked = jnp.concatenate([high, low], axis=0)
        prod = jnp.dot(stacked, ham[...], preferred_element_type=F32)
        prod += lax.dot_general(stacked, ham[...], LAST, preferred_element_type=F32)
        return factor * (0.5 * (prod[:own] + prod[own:]) + diag_all * panel)

    def cubic(panel):
        return 0.5 * (3.0 * panel - times(times(panel)))

    start = pl.multiple_of(me * own, own)
    turned = lax.dot_general(
        eye.astype(BF16), ham[:, pl.ds(start, own)], LAST, preferred_element_type=F32
    )
    across = ham[pl.ds(start, own), :].astype(F32)
    wide_rows = lax.broadcasted_iota(jnp.int32, (own, width), 0)
    wide_cols = lax.broadcasted_iota(jnp.int32, (own, width), 1)
    on_diag = wide_cols == wide_rows + start
    first = 0.5 * (turned + across) + jnp.where(on_diag, diag_all, 0.0)
    left = cubic(factor * first)
    inner = lax.fori_loop(0, 2, lambda _, panel: cubic(times(panel)), left)
    out_ref[...] = (0.5 * (3.0 * left - inner)).astype(BF16)


def sign_rows(shards, me, active, mask_row, diag_row):
    count = len(shards)
    width, own = shards[0].shape
    mask_col = jnp.broadcast_to(mask_row[:, None], (width, own)).astype(BF16)
    vmem = pl.BlockSpec(memory_space=pltpu.VMEM)
    smem = pl.BlockSpec(memory_space=pltpu.SMEM)
    return pl.pallas_call(
        lambda *refs: sign_kernel(count, *refs),
        out_shape=jax.ShapeDtypeStruct((own, width), BF16),
        in_specs=[smem, smem] + [vmem] * (3 + count),
        out_specs=vmem,
        scratch_shapes=[pltpu.VMEM((width, width), BF16)],
        compiler_params=pltpu.CompilerParams(vmem_limit_bytes=56 * 2**20),
        cost_estimate=pl.CostEstimate(
            flops=70 * own * width * width, bytes_accessed=2 * width * width, transcendentals=0
        ),
        name="sign_rows",
    )(me, active, mask_col, mask_row.astype(BF16)[None], diag_row[None], *shards)


def returned_kernel(count, above, below, *refs):
    signs = refs[:count]
    up_ref, down_ref = refs[count:]
    own = above.shape[0]
    for k in range(count):
        cols = slice(k * own, (k + 1) * own)
        up_ref[:, cols] = lax.dot_general(
            above[...], signs[k][...], LAST, preferred_element_type=F32
        )
        down_ref[:, cols] = lax.dot_general(
            below[...], signs[k][...], LAST, preferred_element_type=F32
        )


def returned(above, below, signs):
    count = len(signs)
    own, width = above.shape
    vmem = pl.BlockSpec(memory_space=pltpu.VMEM)
    shape = jax.ShapeDtypeStruct((own, count * own), F32)
    return pl.pallas_call(
        lambda *refs: returned_kernel(count, *refs),
        out_shape=(shape, shape),
        in_specs=[vmem] * (2 + count),
        out_specs=(vmem, vmem),
        compiler_params=pltpu.CompilerParams(vmem_limit_bytes=48 * 2**20),
        cost_estimate=pl.CostEstimate(
            flops=4 * own * width * own * count,
            bytes_accessed=2 * own * width * count,
            transcendentals=0,
        ),
        name="returned",
    )(above, below, *signs)


def final_kernel(count, chunks, me_ref, inv, *refs):
    signs = refs[:count]
    lower = refs[count : count + chunks]
    upper = refs[count + chunks : count + 2 * chunks]
    out_ref = refs[-1]
    own = inv.shape[0]
    per = count // chunks
    for k in range(count):
        start = pl.multiple_of((me_ref[0] ^ k) * own, own)
        cols = slice((k % per) * own, (k % per + 1) * own)
        out_ref[:, 0, pl.ds(start, own)] = lower[k // per][:, cols]
        out_ref[:, 1, pl.ds(start, own)] = lax.dot_general(
            inv[...], signs[k][...], LAST, preferred_element_type=F32
        )
        out_ref[:, 2, pl.ds(start, own)] = upper[k // per][:, cols]


def final(me, inv, signs, lower, upper):
    count = len(signs)
    own, width = inv.shape
    vmem = pl.BlockSpec(memory_space=pltpu.VMEM)
    smem = pl.BlockSpec(memory_space=pltpu.SMEM)
    return pl.pallas_call(
        lambda *refs: final_kernel(count, len(lower), *refs),
        out_shape=jax.ShapeDtypeStruct((own, 3, width), F32),
        in_specs=[smem] + [vmem] * (1 + count + 2 * len(lower)),
        out_specs=vmem,
        compiler_params=pltpu.CompilerParams(vmem_limit_bytes=48 * 2**20),
        cost_estimate=pl.CostEstimate(
            flops=2 * own * width * width, bytes_accessed=20 * own * width, transcendentals=0
        ),
        name="final",
    )(me, inv, *signs, *lower, *upper)


def shards(hamiltonian, pattern, onsite, members, orders, intersection_inv):
    slot_count = lax.axis_size("col")
    team_count = lax.axis_size("row")
    team_index = lax.axis_index("row")
    slot_index = lax.axis_index("col")
    team_blocks = slot_count * OWN_BLOCKS
    me = slot_index.astype(jnp.int32)[None]
    up = [(i, (i + 1) % team_count) for i in range(team_count)]
    down = [(j, i) for i, j in up]

    weights = jnp.broadcast_to(
        pattern.astype(F32)[:, None, :, None],
        (pattern.shape[0], BLOCK, pattern.shape[1], BLOCK),
    ).reshape(hamiltonian.shape)
    masked = (hamiltonian * weights).astype(BF16)
    parts = gather_col(masked)

    above = lax.ppermute(intersection_inv[:, 0, :], "row", down)
    below = lax.ppermute(intersection_inv[:, 2, :], "row", up)
    middle = intersection_inv[:, 1, :]

    group = team_index * slot_count + slot_index
    group_members = lax.dynamic_index_in_dim(members, group, 0, keepdims=False)
    group_order = lax.dynamic_index_in_dim(orders, group, 0, keepdims=False)
    chosen = (group_members[None, :] == jnp.arange(team_blocks, dtype=jnp.int32)[:, None]) & (
        jnp.arange(members.shape[1])[None, :] < group_order
    )
    mask_row = jnp.repeat(jnp.any(chosen, axis=1).astype(F32), BLOCK)
    diag_row = onsite * mask_row
    signs = sign_rows(parts, me, group_order[None], mask_row, diag_row)

    all_signs = gather_col(signs)
    order = [k for k in range(slot_count) if k % INNER == 0 or k == 1]
    order += [k for k in range(slot_count) if k % INNER == 1 and k != 1]
    half = slot_count // 2
    lower, upper = [], []
    for chunk in (range(half), range(half, slot_count)):
        to_up, to_down = returned(above, below, [all_signs[k] for k in chunk])
        lower.append(lax.ppermute(to_up, "row", up))
        upper.append(lax.ppermute(to_down, "row", down))
    return final(me, middle, all_signs, lower, upper)


def solution(mesh):
    in_specs = (P("row", "col"), P("row", "col"), P("row"), P(), P(), P(("row", "col"), None, None))
    out_specs = P(("row", "col"), None, None)
    return jax.shard_map(shards, mesh=mesh, in_specs=in_specs, out_specs=out_specs, check_vma=False)
```

```python
import jax
import jax.numpy as jnp
from jax import lax
from jax.experimental import pallas as pl
from jax.experimental.pallas import tpu as pltpu
from jax.sharding import PartitionSpec as P

BLOCK = 32
OWN_BLOCKS = 4
AXES = ("row", "col")
F32 = jnp.float32
BF16 = jnp.bfloat16
LAST = (((1,), (1,)), ((), ()))
VMEM = pl.BlockSpec(memory_space=pltpu.VMEM)
SMEM = pl.BlockSpec(memory_space=pltpu.SMEM)


class Place:
    def __init__(self):
        self.rows = lax.axis_size("row")
        self.cols = lax.axis_size("col")
        self.half = self.cols // 2
        self.devices = [(r, c) for r in range(self.rows) for c in range(self.cols)]

    def work(self, row, col):
        upper = col // self.half
        return (row - row % 2 + upper, col ^ ((row % 2 ^ upper) * self.half))

    def send(self, array, target):
        moves = []
        for row, col in self.devices:
            to_row, to_col = target(row, col)
            moves.append((row * self.cols + col, to_row % self.rows * self.cols + to_col))
        return lax.ppermute(array, AXES, moves)


def prepare_kernel(ham_ref, pattern_ref, out_ref):
    across, blocks = pattern_ref.shape
    width = out_ref.shape[1]
    lane = lax.broadcasted_iota(jnp.int32, (across, width), 1) // BLOCK
    spread = (lane == lax.broadcasted_iota(jnp.int32, (across, width), 0)).astype(F32)
    weights = lax.dot_general(
        pattern_ref[...].astype(F32), spread, (((0,), (0,)), ((), ())), preferred_element_type=F32
    )
    for a in range(blocks):
        rows = slice(a * BLOCK, (a + 1) * BLOCK)
        out_ref[rows, :] = (ham_ref[rows, :] * weights[a : a + 1, :]).astype(BF16)


def prepare(hamiltonian, pattern):
    return pl.pallas_call(
        prepare_kernel,
        out_shape=jax.ShapeDtypeStruct(hamiltonian.shape, BF16),
        in_specs=[VMEM, VMEM],
        out_specs=VMEM,
        name="prepare",
    )(hamiltonian, pattern.T)


def sign_kernel(count, slot_ref, active_ref, mask_row, diag_row, *refs):
    shards = refs[:count]
    out_ref, ham = refs[count:]
    width = ham.shape[0]
    own = out_ref.shape[0]
    slot = slot_ref[0]
    squares = jnp.zeros((1, own), F32)
    rows = lax.broadcasted_iota(jnp.int32, (own, own), 0)
    cols = lax.broadcasted_iota(jnp.int32, (own, own), 1)
    eye = rows == cols
    mask_col = jnp.broadcast_to(mask_row[...], (own, width)).T.astype(BF16)
    for k in range(count):
        start = pl.multiple_of((slot ^ k) * own, own)
        block = shards[k][...] * mask_col * mask_row[:, pl.ds(start, own)].astype(BF16)
        ham[:, pl.ds(start, own)] = block
        wide = block.astype(F32)
        squares += 0.5 * jnp.sum(wide * wide, axis=0, keepdims=True)
    for k in range(count):
        start = k * own
        diag = diag_row[:, start : start + own]
        across = ham[start : start + own, :]
        down = ham[:, start : start + own]
        both = jnp.dot(across, down, preferred_element_type=F32)
        here = ham[start : start + own, start : start + own].astype(F32)
        entries = 0.5 * both + 2.0 * diag * here
        squares += jnp.sum(jnp.where(eye, entries, 0.0), axis=0, keepdims=True)
        squares += diag * diag
    total = jnp.sum(squares, axis=1, keepdims=True)
    active_rows = active_ref[0].astype(F32) * BLOCK
    factor = jnp.sqrt(active_rows / (4.0 * (total + 1e-06)))
    diag_all = diag_row[...]

    def times(panel):
        high = panel.astype(BF16)
        low = (panel - high.astype(F32)).astype(BF16)
        stacked = jnp.concatenate([high, low], axis=0)
        prod = jnp.dot(stacked, ham[...], preferred_element_type=F32)
        prod += lax.dot_general(stacked, ham[...], LAST, preferred_element_type=F32)
        return factor * (0.5 * (prod[:own] + prod[own:]) + diag_all * panel)

    def cubic(panel):
        return 0.5 * (3.0 * panel - times(times(panel)))

    start = pl.multiple_of(slot * own, own)
    turned = lax.dot_general(
        eye.astype(BF16), ham[:, pl.ds(start, own)], LAST, preferred_element_type=F32
    )
    across = ham[pl.ds(start, own), :].astype(F32)
    wide_rows = lax.broadcasted_iota(jnp.int32, (own, width), 0)
    wide_cols = lax.broadcasted_iota(jnp.int32, (own, width), 1)
    on_diag = wide_cols == wide_rows + start
    first = 0.5 * (turned + across) + jnp.where(on_diag, diag_all, 0.0)
    left = cubic(factor * first)
    inner = lax.fori_loop(0, 2, lambda _, panel: cubic(times(panel)), left, unroll=count <= 8)
    out_ref[...] = (0.5 * (3.0 * left - inner)).astype(BF16)


def sign_rows(shards, slot, active, mask_row, diag_row):
    count = len(shards)
    width, own = shards[0].shape
    return pl.pallas_call(
        lambda *refs: sign_kernel(count, *refs),
        out_shape=jax.ShapeDtypeStruct((own, width), BF16),
        in_specs=[SMEM, SMEM] + [VMEM] * (2 + count),
        out_specs=VMEM,
        scratch_shapes=[pltpu.VMEM((width, width), BF16)],
        compiler_params=pltpu.CompilerParams(vmem_limit_bytes=8 * 2**20 + 11 * width * width),
        cost_estimate=pl.CostEstimate(
            flops=70 * own * width * width, bytes_accessed=2 * width * width, transcendentals=0
        ),
        name="sign_rows",
    )(slot, active, mask_row[None], diag_row[None], *shards)


def products_kernel(count, sides, *refs):
    signs, outs = refs[2 : 2 + count], refs[2 + count :]
    own = signs[0].shape[0]
    for k in range(count):
        cols = slice(k * own, (k + 1) * own)
        for j in range(2):
            prod = lax.dot_general(refs[j][...], signs[k][...], LAST, preferred_element_type=F32)
            for side in range(sides):
                outs[j * sides + side][:, cols] = prod[side * own : (side + 1) * own]


def products(trio, mates, signs):
    count = len(signs)
    own, width = signs[0].shape
    sides = trio.shape[0] // own
    shape = jax.ShapeDtypeStruct((own, count * own), F32)
    return pl.pallas_call(
        lambda *refs: products_kernel(count, sides, *refs),
        out_shape=[shape] * (2 * sides),
        in_specs=[VMEM] * (2 + count),
        out_specs=[VMEM] * (2 * sides),
        compiler_params=pltpu.CompilerParams(vmem_limit_bytes=24 * 2**20),
        cost_estimate=pl.CostEstimate(
            flops=4 * sides * own * width * own * count,
            bytes_accessed=2 * width * own * (2 * sides + count),
            transcendentals=0,
        ),
        name="products",
    )(trio, mates, *signs)


def final_kernel(groups, own, slot_ref, *refs):
    out_ref = refs[-1]
    at = 0
    for steps in groups:
        for side in range(3):
            for mate in range(2):
                part = refs[at]
                at += 1
                for k, step in enumerate(steps):
                    start = pl.multiple_of((slot_ref[0] ^ (step + mate)) * own, own)
                    out_ref[side, :, pl.ds(start, own)] = part[:, k * own : (k + 1) * own]


def final(slot, groups, parts, width):
    flat = [p for part in parts for side in part for p in side]
    own = flat[0].shape[0]
    return pl.pallas_call(
        lambda *refs: final_kernel(groups, own, *refs),
        out_shape=jax.ShapeDtypeStruct((3, own, width), F32),
        in_specs=[SMEM] + [VMEM] * len(flat),
        out_specs=VMEM,
        compiler_params=pltpu.CompilerParams(vmem_limit_bytes=24 * 2**20),
        cost_estimate=pl.CostEstimate(
            flops=0, bytes_accessed=24 * own * width, transcendentals=0
        ),
        name="final",
    )(slot, *flat)


def shards(hamiltonian, pattern, onsite, members, orders, intersection_inv):
    place = Place()
    cols, half = place.cols, place.half
    row, col = lax.axis_index("row"), lax.axis_index("col")
    team, slot = place.work(row, col)
    team_blocks = cols * OWN_BLOCKS
    send = place.send

    def home(r, c):
        return (r, c) if c // half == r % 2 else (r ^ 1, c ^ half)

    masked = prepare(hamiltonian, pattern)
    held = send(masked, home)
    parts = [held]
    for step in range(1, half):
        parts.append(send(held, lambda r, c, step=step: (r, c ^ step)))

    invs = intersection_inv.transpose(1, 0, 2)
    above = send(invs[0], lambda r, c: (r - 1, c))
    below = send(invs[2], lambda r, c: (r + 1, c))

    group = team * cols + slot
    group_members = lax.dynamic_index_in_dim(members, group, 0, keepdims=False)
    group_order = lax.dynamic_index_in_dim(orders, group, 0, keepdims=False)
    chosen = (group_members[None, :] == jnp.arange(team_blocks, dtype=jnp.int32)[:, None]) & (
        jnp.arange(members.shape[1])[None, :] < group_order
    )
    mask_row = jnp.repeat(jnp.any(chosen, axis=1).astype(F32), BLOCK)
    diag_row = onsite_of(onsite, place, team, row) * mask_row
    parts, mask_row, diag_row, above, below = lax.optimization_barrier(
        (parts, mask_row, diag_row, above, below)
    )
    trio = jnp.concatenate([above, invs[1], below], axis=0)
    mates = send(trio, lambda r, c: (r, c ^ 1))
    parts += [send(part, lambda r, c: (r ^ 1, c)) for part in parts]
    signs = sign_rows(
        parts, slot.astype(jnp.int32)[None], group_order[None], mask_row, diag_row
    )

    mine = []
    for step in range(0, cols, 2):

        def target(r, c, step=step):
            team, slot = place.work(r, c)
            return (team, slot ^ step)

        mine.append(send(signs, target))
    order = sorted(range(half), key=lambda k: k % 2)
    groups, placed = [], []
    for chosen_steps in (order[: half // 2], order[half // 2 :]):
        groups.append([2 * k for k in chosen_steps])
        out = products(trio, mates, [mine[k] for k in chosen_steps])
        placed.append(
            [
                [
                    send(out[0], lambda r, c: (r + 1, c)),
                    send(out[3], lambda r, c: (r + 1, c ^ 1)),
                ],
                [out[1], send(out[4], lambda r, c: (r, c ^ 1))],
                [
                    send(out[2], lambda r, c: (r - 1, c)),
                    send(out[5], lambda r, c: (r - 1, c ^ 1)),
                ],
            ]
        )
    width = cols * hamiltonian.shape[1]
    result = final(col.astype(jnp.int32)[None], groups, placed, width)
    return result.transpose(1, 0, 2)


def onsite_of(onsite, place, team, row):
    other = place.send(onsite, lambda r, c: (r ^ 1, c))
    return jnp.where(team == row, onsite, other)


def solution(mesh):
    in_specs = (P("row", "col"), P("row", "col"), P("row"), P(), P(), P(("row", "col"), None, None))
    out_specs = P(("row", "col"), None, None)
    return jax.shard_map(shards, mesh=mesh, in_specs=in_specs, out_specs=out_specs, check_vma=False)
```

```python
import jax
import jax.numpy as jnp
from jax import lax
from jax.experimental import pallas as pl
from jax.experimental.pallas import tpu as pltpu
from jax.sharding import PartitionSpec as P

BLOCK = 32
OWN_BLOCKS = 4
AXES = ("row", "col")
F32 = jnp.float32
BF16 = jnp.bfloat16
LAST = (((1,), (1,)), ((), ()))
LARGEST = 0.09375
CODES = 32766.0
VMEM = pl.BlockSpec(memory_space=pltpu.VMEM)
SMEM = pl.BlockSpec(memory_space=pltpu.SMEM)


class Place:
    def __init__(self):
        self.rows = lax.axis_size("row")
        self.cols = lax.axis_size("col")
        self.half = self.cols // 2
        self.devices = [(r, c) for r in range(self.rows) for c in range(self.cols)]

    def work(self, row, col):
        upper = col // self.half
        return (row - row % 2 + upper, col ^ ((row % 2 ^ upper) * self.half))

    def send(self, array, target):
        moves = []
        for row, col in self.devices:
            to_row, to_col = target(row, col)
            moves.append((row * self.cols + col, to_row % self.rows * self.cols + to_col))
        return lax.ppermute(array, AXES, moves)


def prepare_kernel(ham_ref, pattern_ref, out_ref):
    across, blocks = pattern_ref.shape
    width = out_ref.shape[1]
    lane = lax.broadcasted_iota(jnp.int32, (across, width), 1) // BLOCK
    spread = (lane == lax.broadcasted_iota(jnp.int32, (across, width), 0)).astype(F32)
    weights = lax.dot_general(
        pattern_ref[...].astype(F32), spread, (((0,), (0,)), ((), ())), preferred_element_type=F32
    )
    for a in range(blocks):
        rows = slice(a * BLOCK, (a + 1) * BLOCK)
        entry = ham_ref[rows, :] * weights[a : a + 1, :]
        root = jnp.sqrt(jnp.sqrt(jnp.abs(entry) * (1.0 / LARGEST)))
        code = (root * CODES + 0.5).astype(jnp.int32)
        out_ref[rows, :] = jnp.where(entry < 0.0, -code, code).astype(jnp.int16)


def prepare(hamiltonian, pattern):
    return pl.pallas_call(
        prepare_kernel,
        out_shape=jax.ShapeDtypeStruct(hamiltonian.shape, jnp.int16),
        in_specs=[VMEM, VMEM],
        out_specs=VMEM,
        compiler_params=pltpu.CompilerParams(vmem_limit_bytes=8 * 2**20),
        name="prepare",
    )(hamiltonian, pattern.T)


def sign_kernel(count, slot_ref, active_ref, mask_row, diag_row, *refs):
    shards = refs[:count]
    out_ref, ham, high_ref, low_ref = refs[count:]
    width = ham.shape[0]
    own = out_ref.shape[0]
    slot = slot_ref[0]
    mask_col = jnp.broadcast_to(mask_row[...], (own, width)).T
    for k in range(count):
        start = pl.multiple_of((slot ^ k) * own, own)
        root = shards[k][...].astype(F32) * (1.0 / CODES)
        entry = (root * jnp.abs(root)) * (root * root) * LARGEST
        ham[:, pl.ds(start, own)] = entry * mask_col * mask_row[:, pl.ds(start, own)]
    rows = lax.broadcasted_iota(jnp.int32, (own, width), 0)
    cols = lax.broadcasted_iota(jnp.int32, (own, width), 1)

    def strip(k, squares):
        at = pl.ds(pl.multiple_of(k * own, own), own)
        diag = jnp.where(cols == rows + k * own, diag_row[...], 0.0)
        both = 0.5 * (ham[at, :] + ham[:, at].T) + diag
        high = both.astype(BF16)
        high_ref[at, :] = high
        low_ref[at, :] = (both - high.astype(F32)).astype(BF16)
        return squares + jnp.sum(both * both, axis=0, keepdims=True)

    small = count <= 8
    squares = lax.fori_loop(0, count, strip, jnp.zeros((1, width), F32), unroll=small)
    total = jnp.sum(squares, axis=1, keepdims=True)
    active_rows = active_ref[0].astype(F32) * BLOCK
    factor = jnp.sqrt(active_rows / (4.0 * (total + 1e-06)))

    def times(panel):
        high = panel.astype(BF16)
        low = (panel - high.astype(F32)).astype(BF16)
        stacked = jnp.concatenate([high, low], axis=0)
        prod = jnp.dot(stacked, high_ref[...], preferred_element_type=F32)
        rest = jnp.dot(high, low_ref[...], preferred_element_type=F32)
        return factor * (prod[:own] + prod[own:] + rest)

    def cubic(panel):
        return 0.5 * (3.0 * panel - times(times(panel)))

    at = pl.ds(pl.multiple_of(slot * own, own), own)
    first = high_ref[at, :].astype(F32) + low_ref[at, :].astype(F32)
    left = cubic(factor * first)
    inner = lax.fori_loop(0, 2, lambda _, panel: cubic(times(panel)), left, unroll=small)
    out_ref[...] = (0.5 * (3.0 * left - inner)).astype(BF16)


def sign_rows(shards, slot, active, mask_row, diag_row):
    count = len(shards)
    width, own = shards[0].shape
    return pl.pallas_call(
        lambda *refs: sign_kernel(count, *refs),
        out_shape=jax.ShapeDtypeStruct((own, width), BF16),
        in_specs=[SMEM, SMEM] + [VMEM] * (2 + count),
        out_specs=VMEM,
        scratch_shapes=[
            pltpu.VMEM((width, width), F32),
            pltpu.VMEM((width, width), BF16),
            pltpu.VMEM((width, width), BF16),
        ],
        compiler_params=pltpu.CompilerParams(vmem_limit_bytes=8 * 2**20 + 12 * width * width),
        cost_estimate=pl.CostEstimate(
            flops=70 * own * width * width, bytes_accessed=2 * width * width, transcendentals=0
        ),
        name="sign_rows",
    )(slot, active, mask_row[None], diag_row[None], *shards)


def products_kernel(count, sides, *refs):
    signs, outs = refs[2 : 2 + count], refs[2 + count :]
    own = signs[0].shape[0]
    for k in range(count):
        cols = slice(k * own, (k + 1) * own)
        for j in range(2):
            prod = lax.dot_general(refs[j][...], signs[k][...], LAST, preferred_element_type=F32)
            for side in range(sides):
                out = outs[j * sides + side]
                out[:, cols] = prod[side * own : (side + 1) * own].astype(out.dtype)


def products(trio, mates, signs):
    count = len(signs)
    own, width = signs[0].shape
    sides = trio.shape[0] // own
    kinds = [F32 if k == 1 else BF16 for k in range(2 * sides)]
    return pl.pallas_call(
        lambda *refs: products_kernel(count, sides, *refs),
        out_shape=[jax.ShapeDtypeStruct((own, count * own), kind) for kind in kinds],
        in_specs=[VMEM] * (2 + count),
        out_specs=[VMEM] * (2 * sides),
        compiler_params=pltpu.CompilerParams(vmem_limit_bytes=24 * 2**20),
        cost_estimate=pl.CostEstimate(
            flops=4 * sides * own * width * own * count,
            bytes_accessed=2 * width * own * (2 * sides + count),
            transcendentals=0,
        ),
        name="products",
    )(trio, mates, *signs)


def final_kernel(groups, own, slot_ref, *refs):
    out_ref = refs[-1]
    at = 0
    for steps in groups:
        for side in range(3):
            for mate in range(2):
                part = refs[at]
                at += 1
                for k, step in enumerate(steps):
                    start = pl.multiple_of((slot_ref[0] ^ (step + mate)) * own, own)
                    block = part[:, k * own : (k + 1) * own]
                    out_ref[side, :, pl.ds(start, own)] = block.astype(F32)


def final(slot, groups, parts, width):
    flat = [p for part in parts for side in part for p in side]
    own = flat[0].shape[0]
    return pl.pallas_call(
        lambda *refs: final_kernel(groups, own, *refs),
        out_shape=jax.ShapeDtypeStruct((3, own, width), F32),
        in_specs=[SMEM] + [VMEM] * len(flat),
        out_specs=VMEM,
        compiler_params=pltpu.CompilerParams(vmem_limit_bytes=24 * 2**20),
        cost_estimate=pl.CostEstimate(
            flops=0, bytes_accessed=24 * own * width, transcendentals=0
        ),
        name="final",
    )(slot, *flat)


def shards(hamiltonian, pattern, onsite, members, orders, intersection_inv):
    place = Place()
    cols, half = place.cols, place.half
    row, col = lax.axis_index("row"), lax.axis_index("col")
    team, slot = place.work(row, col)
    team_blocks = cols * OWN_BLOCKS
    send = place.send

    def home(r, c):
        return (r, c) if c // half == r % 2 else (r ^ 1, c ^ half)

    masked = prepare(hamiltonian, pattern)
    masked, onsite = lax.optimization_barrier((masked, onsite))
    held = send(masked, home)
    parts = [held]
    for step in range(1, half):
        parts.append(send(held, lambda r, c, step=step: (r, c ^ step)))

    invs = intersection_inv.transpose(1, 0, 2)
    above = send(invs[0], lambda r, c: (r - 1, c))
    below = send(invs[2], lambda r, c: (r + 1, c))

    group = team * cols + slot
    group_members = lax.dynamic_index_in_dim(members, group, 0, keepdims=False)
    group_order = lax.dynamic_index_in_dim(orders, group, 0, keepdims=False)
    chosen = (group_members[None, :] == jnp.arange(team_blocks, dtype=jnp.int32)[:, None]) & (
        jnp.arange(members.shape[1])[None, :] < group_order
    )
    mask_row = jnp.repeat(jnp.any(chosen, axis=1).astype(F32), BLOCK)
    diag_row = onsite_of(onsite, place, team, row) * mask_row
    parts, mask_row, diag_row, above, below = lax.optimization_barrier(
        (parts, mask_row, diag_row, above, below)
    )
    trio = jnp.concatenate([above, invs[1], below], axis=0)
    mates = send(trio, lambda r, c: (r, c ^ 1))
    parts += [send(part, lambda r, c: (r ^ 1, c)) for part in parts]
    signs = sign_rows(
        parts, slot.astype(jnp.int32)[None], group_order[None], mask_row, diag_row
    )

    mine = []
    for step in range(0, cols, 2):

        def target(r, c, step=step):
            team, slot = place.work(r, c)
            return (team, slot ^ step)

        mine.append(send(signs, target))
    order = sorted(range(half), key=lambda k: k % 2)
    groups, placed = [], []
    for chosen_steps in (order[: half // 2], order[half // 2 :]):
        groups.append([2 * k for k in chosen_steps])
        out = products(trio, mates, [mine[k] for k in chosen_steps])
        placed.append(
            [
                [
                    send(out[0], lambda r, c: (r + 1, c)),
                    send(out[3], lambda r, c: (r + 1, c ^ 1)),
                ],
                [out[1], send(out[4], lambda r, c: (r, c ^ 1))],
                [
                    send(out[2], lambda r, c: (r - 1, c)),
                    send(out[5], lambda r, c: (r - 1, c ^ 1)),
                ],
            ]
        )
    width = cols * hamiltonian.shape[1]
    result = final(col.astype(jnp.int32)[None], groups, placed, width)
    return result.transpose(1, 0, 2)


def onsite_of(onsite, place, team, row):
    other = place.send(onsite, lambda r, c: (r ^ 1, c))
    return jnp.where(team == row, onsite, other)


def solution(mesh):
    in_specs = (P("row", "col"), P("row", "col"), P("row"), P(), P(), P(("row", "col"), None, None))
    out_specs = P(("row", "col"), None, None)
    return jax.shard_map(shards, mesh=mesh, in_specs=in_specs, out_specs=out_specs, check_vma=False)
```

```python
import jax
import jax.numpy as jnp
from jax import lax
from jax.experimental import pallas as pl
from jax.experimental.pallas import tpu as pltpu
from jax.sharding import PartitionSpec as P

BLOCK = 32
OWN_BLOCKS = 4
AXES = ("row", "col")
F32 = jnp.float32
BF16 = jnp.bfloat16
LAST = (((1,), (1,)), ((), ()))
LARGEST = 0.09375
CODES = 32766.0
VMEM = pl.BlockSpec(memory_space=pltpu.VMEM)
HBM = pl.BlockSpec(memory_space=pltpu.HBM)
SMEM = pl.BlockSpec(memory_space=pltpu.SMEM)


class Place:
    def __init__(self):
        self.rows = lax.axis_size("row")
        self.cols = lax.axis_size("col")
        self.half = self.cols // 2
        self.devices = [(r, c) for r in range(self.rows) for c in range(self.cols)]

    def work(self, row, col):
        upper = col // self.half
        return (row - row % 2 + upper, col ^ ((row % 2 ^ upper) * self.half))

    def send(self, array, target):
        moves = []
        for row, col in self.devices:
            if target(row, col) is None:
                continue
            to_row, to_col = target(row, col)
            moves.append((row * self.cols + col, to_row % self.rows * self.cols + to_col))
        return lax.ppermute(array, AXES, moves)


def prepare_kernel(pieces, ham_hbm, pattern_hbm, out_hbm, ham, pattern, out, in_sems, out_sems):
    across, blocks = pattern.shape
    height, width = ham.shape
    part = height // pieces
    incoming = [pltpu.make_async_copy(pattern_hbm, pattern, in_sems.at[pieces])]
    outgoing = []
    for p in range(pieces):
        rows = pl.ds(p * part, part)
        incoming.append(pltpu.make_async_copy(ham_hbm.at[rows], ham.at[rows], in_sems.at[p]))
        outgoing.append(pltpu.make_async_copy(out.at[rows], out_hbm.at[rows], out_sems.at[p]))
    for copy in incoming:
        copy.start()
    incoming[0].wait()
    lane = lax.broadcasted_iota(jnp.int32, (across, width), 1) // BLOCK
    spread = (lane == lax.broadcasted_iota(jnp.int32, (across, width), 0)).astype(F32)
    weights = lax.dot_general(
        pattern[...].astype(F32), spread, (((0,), (0,)), ((), ())), preferred_element_type=F32
    )
    for p in range(pieces):
        incoming[p + 1].wait()
        for a in range(p * blocks // pieces, (p + 1) * blocks // pieces):
            rows = slice(a * BLOCK, (a + 1) * BLOCK)
            entry = ham[rows, :] * weights[a : a + 1, :]
            root = jnp.sqrt(jnp.sqrt(jnp.abs(entry) * (1.0 / LARGEST)))
            code = (root * CODES + 0.5).astype(jnp.int32)
            out[rows, :] = jnp.where(entry < 0.0, -code, code).astype(jnp.int16)
        outgoing[p].start()
    for copy in outgoing:
        copy.wait()


def prepare(hamiltonian, pattern):
    pieces = 4
    return pl.pallas_call(
        lambda *refs: prepare_kernel(pieces, *refs),
        out_shape=jax.ShapeDtypeStruct(hamiltonian.shape, jnp.int16),
        in_specs=[HBM, HBM],
        out_specs=HBM,
        scratch_shapes=[
            pltpu.VMEM(hamiltonian.shape, F32),
            pltpu.VMEM(pattern.shape[::-1], jnp.int32),
            pltpu.VMEM(hamiltonian.shape, jnp.int16),
            pltpu.SemaphoreType.DMA((pieces + 1,)),
            pltpu.SemaphoreType.DMA((pieces,)),
        ],
        name="prepare",
    )(hamiltonian, pattern.T)


def sign_kernel(count, slot_ref, active_ref, mask_row, diag_row, *refs):
    shards = refs[:count]
    out_ref, ham, high_ref, low_ref = refs[count:]
    width = ham.shape[0]
    own = out_ref.shape[0]
    slot = slot_ref[0]
    mask_col = jnp.broadcast_to(mask_row[...], (own, width)).T
    for k in range(count):
        start = pl.multiple_of((slot ^ k) * own, own)
        root = shards[k][...].astype(F32) * (1.0 / CODES)
        entry = (root * jnp.abs(root)) * (root * root) * LARGEST
        ham[:, pl.ds(start, own)] = entry * mask_col * mask_row[:, pl.ds(start, own)]
    rows = lax.broadcasted_iota(jnp.int32, (own, width), 0)
    cols = lax.broadcasted_iota(jnp.int32, (own, width), 1)

    def strip(k, squares):
        at = pl.ds(pl.multiple_of(k * own, own), own)
        diag = jnp.where(cols == rows + k * own, diag_row[...], 0.0)
        both = 0.5 * (ham[at, :] + ham[:, at].T) + diag
        high = both.astype(BF16)
        high_ref[at, :] = high
        low_ref[at, :] = (both - high.astype(F32)).astype(BF16)
        return squares + jnp.sum(both * both, axis=0, keepdims=True)

    small = count <= 8
    squares = lax.fori_loop(0, count, strip, jnp.zeros((1, width), F32), unroll=small)
    total = jnp.sum(squares, axis=1, keepdims=True)
    active_rows = active_ref[0].astype(F32) * BLOCK
    factor = jnp.sqrt(active_rows / (4.0 * (total + 1e-06)))

    def times(panel):
        high = panel.astype(BF16)
        low = (panel - high.astype(F32)).astype(BF16)
        stacked = jnp.concatenate([high, low], axis=0)
        prod = jnp.dot(stacked, high_ref[...], preferred_element_type=F32)
        rest = jnp.dot(high, low_ref[...], preferred_element_type=F32)
        return factor * (prod[:own] + prod[own:] + rest)

    def cubic(panel):
        return 0.5 * (3.0 * panel - times(times(panel)))

    at = pl.ds(pl.multiple_of(slot * own, own), own)
    first = high_ref[at, :].astype(F32) + low_ref[at, :].astype(F32)
    left = cubic(factor * first)
    inner = lax.fori_loop(0, 2, lambda _, panel: cubic(times(panel)), left, unroll=small)
    out_ref[...] = (0.5 * (3.0 * left - inner)).astype(BF16)


def sign_rows(shards, slot, active, mask_row, diag_row):
    count = len(shards)
    width, own = shards[0].shape
    return pl.pallas_call(
        lambda *refs: sign_kernel(count, *refs),
        out_shape=jax.ShapeDtypeStruct((own, width), BF16),
        in_specs=[SMEM, SMEM] + [VMEM] * (2 + count),
        out_specs=VMEM,
        scratch_shapes=[
            pltpu.VMEM((width, width), F32),
            pltpu.VMEM((width, width), BF16),
            pltpu.VMEM((width, width), BF16),
        ],
        compiler_params=pltpu.CompilerParams(vmem_limit_bytes=8 * 2**20 + 12 * width * width),
        cost_estimate=pl.CostEstimate(
            flops=70 * own * width * width, bytes_accessed=2 * width * width, transcendentals=0
        ),
        name="sign_rows",
    )(slot, active, mask_row[None], diag_row[None], *shards)


def products_kernel(sources, sides, *refs):
    signs, outs = refs[2 : -2 * sides], refs[-2 * sides :]
    own = outs[0].shape[0]
    for k, source in enumerate(sources):
        cols = slice(k * own, (k + 1) * own)
        shard = sum(signs[i][j * own : (j + 1) * own, :] for i, j in source)
        for j in range(2):
            prod = lax.dot_general(refs[j][...], shard, LAST, preferred_element_type=F32)
            for side in range(sides):
                out = outs[j * sides + side]
                out[:, cols] = prod[side * own : (side + 1) * own].astype(out.dtype)


def products(trio, mates, sources, own):
    arrays = []
    for source in sources:
        arrays += [a for a, _ in source if all(a is not b for b in arrays)]
    indices = [
        [(next(i for i, b in enumerate(arrays) if b is a), j) for a, j in source]
        for source in sources
    ]
    count, width = len(sources), trio.shape[1]
    sides = trio.shape[0] // own
    kinds = [F32 if k == 1 else BF16 for k in range(2 * sides)]
    return pl.pallas_call(
        lambda *refs: products_kernel(indices, sides, *refs),
        out_shape=[jax.ShapeDtypeStruct((own, count * own), kind) for kind in kinds],
        in_specs=[VMEM] * (2 + len(arrays)),
        out_specs=[VMEM] * (2 * sides),
        compiler_params=pltpu.CompilerParams(vmem_limit_bytes=24 * 2**20),
        cost_estimate=pl.CostEstimate(
            flops=4 * sides * own * width * own * count,
            bytes_accessed=2 * width * own * (2 * sides + count),
            transcendentals=0,
        ),
        name="products",
    )(trio, mates, *arrays)


def final_kernel(groups, own, slot_ref, *refs):
    out_hbm, out_ref, sems = refs[-3:]
    copies = []
    for side in range(3):
        for group, steps in enumerate(groups):
            for mate in range(2):
                part = refs[(group * 3 + side) * 2 + mate]
                for k, step in enumerate(steps):
                    start = pl.multiple_of((slot_ref[0] ^ (step + mate)) * own, own)
                    block = part[:, k * own : (k + 1) * own]
                    out_ref[side, :, pl.ds(start, own)] = block.astype(F32)
        copies.append(pltpu.make_async_copy(out_ref.at[side], out_hbm.at[side], sems.at[side]))
        copies[side].start()
    for copy in copies:
        copy.wait()


def final(slot, groups, parts, width):
    flat = [p for part in parts for side in part for p in side]
    own = flat[0].shape[0]
    return pl.pallas_call(
        lambda *refs: final_kernel(groups, own, *refs),
        out_shape=jax.ShapeDtypeStruct((3, own, width), F32),
        in_specs=[SMEM] + [VMEM] * len(flat),
        out_specs=HBM,
        scratch_shapes=[pltpu.VMEM((3, own, width), F32), pltpu.SemaphoreType.DMA((3,))],
        compiler_params=pltpu.CompilerParams(vmem_limit_bytes=24 * 2**20),
        cost_estimate=pl.CostEstimate(
            flops=0, bytes_accessed=24 * own * width, transcendentals=0
        ),
        name="final",
    )(slot, *flat)


def shards(hamiltonian, pattern, onsite, members, orders, intersection_inv):
    place = Place()
    cols, half = place.cols, place.half
    row, col = lax.axis_index("row"), lax.axis_index("col")
    team, slot = place.work(row, col)
    team_blocks = cols * OWN_BLOCKS
    send = place.send

    def home(r, c):
        return (r, c) if c // half == r % 2 else (r ^ 1, c ^ half)

    masked = prepare(hamiltonian, pattern)
    held = send(masked, home)
    held, onsite = lax.optimization_barrier((held, onsite))
    parts = [held]
    for step in range(1, half):
        parts.append(send(held, lambda r, c, step=step: (r, c ^ step)))

    invs = intersection_inv.transpose(1, 0, 2)
    above = send(invs[0], lambda r, c: (r - 1, c))
    below = send(invs[2], lambda r, c: (r + 1, c))

    group = team * cols + slot
    group_members = lax.dynamic_index_in_dim(members, group, 0, keepdims=False)
    group_order = lax.dynamic_index_in_dim(orders, group, 0, keepdims=False)
    chosen = (group_members[None, :] == jnp.arange(team_blocks, dtype=jnp.int32)[:, None]) & (
        jnp.arange(members.shape[1])[None, :] < group_order
    )
    mask_row = jnp.repeat(jnp.any(chosen, axis=1).astype(F32), BLOCK)
    diag_row = onsite_of(onsite, place, team, row) * mask_row
    parts += [send(part, lambda r, c: (r ^ 1, c)) for part in parts]
    last, mask_row, diag_row, above, below = lax.optimization_barrier(
        (parts[half - 1], mask_row, diag_row, above, below)
    )
    parts[half - 1] = last
    trio = jnp.concatenate([above, invs[1], below], axis=0)
    mates = send(trio, lambda r, c: (r, c ^ 1))
    signs = sign_rows(
        parts, slot.astype(jnp.int32)[None], group_order[None], mask_row, diag_row
    )

    def at_step(step, within):
        def target(r, c):
            team, slot = place.work(r, c)
            same = (slot ^ step) // half == c // half
            return (team, slot ^ step) if same or not within else None

        return target

    def onward(step):
        return lambda r, c: (r, c ^ step) if c // half != r % 2 else None

    steps = range(2, half, 2)
    first = [send(signs, at_step(0, False)), send(signs, at_step(half, False))]
    near = [[send(signs, at_step(k ^ j, True)) for j in (0, half)] for k in steps]
    pair, near, mates = lax.optimization_barrier((jnp.concatenate(first, axis=0), near, mates))
    far = [send(pair, onward(k)) for k in steps]
    own = signs.shape[0]
    groups, sources = [[0, half]], [[[(part, 0)] for part in first]]
    groups.append([k ^ j for k in steps for j in (0, half)])
    sources.append(
        [[(near[i][j], 0), (far[i], j)] for i in range(len(near)) for j in range(2)]
    )
    placed = []
    for source in sources:
        out = products(trio, mates, source, own)
        placed.append(
            [
                [
                    send(out[0], lambda r, c: (r + 1, c)),
                    send(out[3], lambda r, c: (r + 1, c ^ 1)),
                ],
                [out[1], send(out[4], lambda r, c: (r, c ^ 1))],
                [
                    send(out[2], lambda r, c: (r - 1, c)),
                    send(out[5], lambda r, c: (r - 1, c ^ 1)),
                ],
            ]
        )
    width = cols * hamiltonian.shape[1]
    result = final(col.astype(jnp.int32)[None], groups, placed, width)
    return result.transpose(1, 0, 2)


def onsite_of(onsite, place, team, row):
    other = place.send(onsite, lambda r, c: (r ^ 1, c))
    return jnp.where(team == row, onsite, other)


def solution(mesh):
    in_specs = (P("row", "col"), P("row", "col"), P("row"), P(), P(), P(("row", "col"), None, None))
    out_specs = P(("row", "col"), None, None)
    return jax.shard_map(shards, mesh=mesh, in_specs=in_specs, out_specs=out_specs, check_vma=False)
```

```python
import jax
import jax.numpy as jnp
from jax import lax
from jax.experimental import pallas as pl
from jax.experimental.pallas import tpu as pltpu
from jax.sharding import PartitionSpec as P

BLOCK = 32
OWN_BLOCKS = 4
AXES = ("row", "col")
F32 = jnp.float32
BF16 = jnp.bfloat16
LAST = (((1,), (1,)), ((), ()))
LARGEST = 0.09375
CODES = 32766.0
VMEM = pl.BlockSpec(memory_space=pltpu.VMEM)
HBM = pl.BlockSpec(memory_space=pltpu.HBM)
SMEM = pl.BlockSpec(memory_space=pltpu.SMEM)


class Place:
    def __init__(self):
        self.rows = lax.axis_size("row")
        self.cols = lax.axis_size("col")
        self.half = self.cols // 2
        self.devices = [(r, c) for r in range(self.rows) for c in range(self.cols)]

    def work(self, row, col):
        upper = col // self.half
        return (row - row % 2 + upper, col ^ ((row % 2 ^ upper) * self.half))

    def send(self, array, target):
        moves = []
        for row, col in self.devices:
            if target(row, col) is None:
                continue
            to_row, to_col = target(row, col)
            moves.append((row * self.cols + col, to_row % self.rows * self.cols + to_col))
        return lax.ppermute(array, AXES, moves)


def prepare_kernel(pieces, ham_hbm, pattern_hbm, out_hbm, ham, pattern, out, in_sems, out_sems):
    across, blocks = pattern.shape
    height, width = ham.shape
    part = height // pieces
    incoming = [pltpu.make_async_copy(pattern_hbm, pattern, in_sems.at[pieces])]
    outgoing = []
    for p in range(pieces):
        rows = pl.ds(p * part, part)
        incoming.append(pltpu.make_async_copy(ham_hbm.at[rows], ham.at[rows], in_sems.at[p]))
        outgoing.append(pltpu.make_async_copy(out.at[rows], out_hbm.at[rows], out_sems.at[p]))
    for copy in incoming:
        copy.start()
    incoming[0].wait()
    lane = lax.broadcasted_iota(jnp.int32, (across, width), 1) // BLOCK
    spread = (lane == lax.broadcasted_iota(jnp.int32, (across, width), 0)).astype(F32)
    weights = lax.dot_general(
        pattern[...].astype(F32), spread, (((0,), (0,)), ((), ())), preferred_element_type=F32
    )
    for p in range(pieces):
        incoming[p + 1].wait()
        for a in range(p * blocks // pieces, (p + 1) * blocks // pieces):
            rows = slice(a * BLOCK, (a + 1) * BLOCK)
            entry = ham[rows, :] * weights[a : a + 1, :]
            root = jnp.sqrt(jnp.sqrt(jnp.abs(entry) * (1.0 / LARGEST)))
            code = (root * CODES + 0.5).astype(jnp.int32)
            out[rows, :] = jnp.where(entry < 0.0, -code, code).astype(jnp.int16)
        outgoing[p].start()
    for copy in outgoing:
        copy.wait()


def prepare(hamiltonian, pattern):
    pieces = 4
    return pl.pallas_call(
        lambda *refs: prepare_kernel(pieces, *refs),
        out_shape=jax.ShapeDtypeStruct(hamiltonian.shape, jnp.int16),
        in_specs=[HBM, HBM],
        out_specs=HBM,
        scratch_shapes=[
            pltpu.VMEM(hamiltonian.shape, F32),
            pltpu.VMEM(pattern.shape[::-1], jnp.int32),
            pltpu.VMEM(hamiltonian.shape, jnp.int16),
            pltpu.SemaphoreType.DMA((pieces + 1,)),
            pltpu.SemaphoreType.DMA((pieces,)),
        ],
        name="prepare",
    )(hamiltonian, pattern.T)


def sign_kernel(count, slot_ref, active_ref, mask_row, diag_row, *refs):
    shards = refs[:count]
    out_ref, ham, high_ref, low_ref = refs[count:]
    width = ham.shape[0]
    own = out_ref.shape[0]
    slot = slot_ref[0]
    mask_col = jnp.broadcast_to(mask_row[...], (own, width)).T
    for k in range(count):
        start = pl.multiple_of((slot ^ k) * own, own)
        root = shards[k][...].astype(F32) * (1.0 / CODES)
        entry = (root * jnp.abs(root)) * (root * root) * LARGEST
        ham[:, pl.ds(start, own)] = entry * mask_col * mask_row[:, pl.ds(start, own)]
    rows = lax.broadcasted_iota(jnp.int32, (own, width), 0)
    cols = lax.broadcasted_iota(jnp.int32, (own, width), 1)

    def strip(k, squares):
        at = pl.ds(pl.multiple_of(k * own, own), own)
        diag = jnp.where(cols == rows + k * own, diag_row[...], 0.0)
        both = 0.5 * (ham[at, :] + ham[:, at].T) + diag
        high = both.astype(BF16)
        high_ref[at, :] = high
        low_ref[at, :] = (both - high.astype(F32)).astype(BF16)
        return squares + jnp.sum(both * both, axis=0, keepdims=True)

    small = count <= 8
    squares = lax.fori_loop(0, count, strip, jnp.zeros((1, width), F32), unroll=small)
    total = jnp.sum(squares, axis=1, keepdims=True)
    active_rows = active_ref[0].astype(F32) * BLOCK
    factor = jnp.sqrt(active_rows / (4.0 * (total + 1e-06)))

    def times(panel):
        high = panel.astype(BF16)
        low = (panel - high.astype(F32)).astype(BF16)
        stacked = jnp.concatenate([high, low], axis=0)
        prod = jnp.dot(stacked, high_ref[...], preferred_element_type=F32)
        rest = jnp.dot(high, low_ref[...], preferred_element_type=F32)
        return factor * (prod[:own] + prod[own:] + rest)

    def cubic(panel):
        return 0.5 * (3.0 * panel - times(times(panel)))

    at = pl.ds(pl.multiple_of(slot * own, own), own)
    first = high_ref[at, :].astype(F32) + low_ref[at, :].astype(F32)
    left = cubic(factor * first)
    inner = lax.fori_loop(0, 2, lambda _, panel: cubic(times(panel)), left, unroll=small)
    out_ref[...] = (0.5 * (3.0 * left - inner)).astype(BF16)


def sign_rows(shards, slot, active, mask_row, diag_row):
    count = len(shards)
    width, own = shards[0].shape
    return pl.pallas_call(
        lambda *refs: sign_kernel(count, *refs),
        out_shape=jax.ShapeDtypeStruct((own, width), BF16),
        in_specs=[SMEM, SMEM] + [VMEM] * (2 + count),
        out_specs=VMEM,
        scratch_shapes=[
            pltpu.VMEM((width, width), F32),
            pltpu.VMEM((width, width), BF16),
            pltpu.VMEM((width, width), BF16),
        ],
        compiler_params=pltpu.CompilerParams(vmem_limit_bytes=6 * 2**20 + 10 * width * width),
        cost_estimate=pl.CostEstimate(
            flops=70 * own * width * width, bytes_accessed=2 * width * width, transcendentals=0
        ),
        name="sign_rows",
    )(slot, active, mask_row[None], diag_row[None], *shards)


def products_kernel(sources, sides, widths, *refs):
    outs = refs[-2 * sides :]
    before = refs[-2 * sides - len(widths) : -2 * sides]
    signs = refs[2 : len(refs) - 2 * sides - len(widths)]
    own = outs[0].shape[0]
    shift = [0] * len(outs)
    for part, side, width in zip(before, (0, 2), widths):
        outs[side][:, :width] = part[...]
        shift[side] = width
    for k, source in enumerate(sources):
        shard = sum(signs[i][j * own : (j + 1) * own, :] for i, j in source)
        for j in range(2):
            prod = lax.dot_general(refs[j][...], shard, LAST, preferred_element_type=F32)
            for side in range(sides):
                out, start = outs[j * sides + side], shift[j * sides + side] + k * own
                block = prod[side * own : (side + 1) * own]
                out[:, start : start + own] = block.astype(out.dtype)


def products(trio, mates, sources, own, before):
    arrays = []
    for source in sources:
        arrays += [a for a, _ in source if all(a is not b for b in arrays)]
    indices = [
        [(next(i for i, b in enumerate(arrays) if b is a), j) for a, j in source]
        for source in sources
    ]
    count, width = len(sources), trio.shape[1]
    sides = trio.shape[0] // own
    shapes = [
        jax.ShapeDtypeStruct((own, count * own), F32 if k == 1 else BF16) for k in range(2 * sides)
    ]
    widths = [part.shape[1] for part in before]
    for part, side in zip(before, (0, 2)):
        shapes[side] = jax.ShapeDtypeStruct((own, count * own + part.shape[1]), BF16)
    return pl.pallas_call(
        lambda *refs: products_kernel(indices, sides, widths, *refs),
        out_shape=shapes,
        in_specs=[VMEM] * (2 + len(arrays) + len(before)),
        out_specs=[VMEM] * (2 * sides),
        compiler_params=pltpu.CompilerParams(vmem_limit_bytes=24 * 2**20),
        cost_estimate=pl.CostEstimate(
            flops=4 * sides * own * width * own * count,
            bytes_accessed=2 * width * own * (2 * sides + count),
            transcendentals=0,
        ),
        name="products",
    )(trio, mates, *arrays, *before)


def final_kernel(places, own, slot_ref, *refs):
    out_hbm, out_ref, sems = refs[-3:]
    copies = []
    for side in (1, 0, 2):
        for part, (at, steps) in zip(refs, places):
            for k, step in enumerate(steps):
                if at == side:
                    start = pl.multiple_of((slot_ref[0] ^ step) * own, own)
                    block = part[:, k * own : (k + 1) * own]
                    out_ref[side, :, pl.ds(start, own)] = block.astype(F32)
        copies.append(pltpu.make_async_copy(out_ref.at[side], out_hbm.at[side], sems.at[side]))
        copies[-1].start()
    for copy in copies:
        copy.wait()


def final(slot, pieces, width):
    places = [(side, steps) for side, steps, _ in pieces]
    flat = [array for _, _, array in pieces]
    own = flat[0].shape[0]
    return pl.pallas_call(
        lambda *refs: final_kernel(places, own, *refs),
        out_shape=jax.ShapeDtypeStruct((3, own, width), F32),
        in_specs=[SMEM] + [VMEM] * len(flat),
        out_specs=HBM,
        scratch_shapes=[pltpu.VMEM((3, own, width), F32), pltpu.SemaphoreType.DMA((3,))],
        compiler_params=pltpu.CompilerParams(vmem_limit_bytes=24 * 2**20),
        cost_estimate=pl.CostEstimate(
            flops=0, bytes_accessed=24 * own * width, transcendentals=0
        ),
        name="final",
    )(slot, *flat)


def shards(hamiltonian, pattern, onsite, members, orders, intersection_inv):
    place = Place()
    cols, half = place.cols, place.half
    row, col = lax.axis_index("row"), lax.axis_index("col")
    team, slot = place.work(row, col)
    team_blocks = cols * OWN_BLOCKS
    send = place.send

    def home(r, c):
        return (r, c) if c // half == r % 2 else (r ^ 1, c ^ half)

    masked = prepare(hamiltonian, pattern)
    held = send(masked, home)
    held, onsite = lax.optimization_barrier((held, onsite))
    parts = [held]
    for step in range(1, half):
        parts.append(send(held, lambda r, c, step=step: (r, c ^ step)))

    invs = intersection_inv.transpose(1, 0, 2)
    above = send(invs[0], lambda r, c: (r - 1, c))
    below = send(invs[2], lambda r, c: (r + 1, c))

    group = team * cols + slot
    group_members = lax.dynamic_index_in_dim(members, group, 0, keepdims=False)
    group_order = lax.dynamic_index_in_dim(orders, group, 0, keepdims=False)
    chosen = (group_members[None, :] == jnp.arange(team_blocks, dtype=jnp.int32)[:, None]) & (
        jnp.arange(members.shape[1])[None, :] < group_order
    )
    mask_row = jnp.repeat(jnp.any(chosen, axis=1).astype(F32), BLOCK)
    diag_row = onsite_of(onsite, place, team, row) * mask_row
    parts += [send(part, lambda r, c: (r ^ 1, c)) for part in parts]
    last, mask_row, diag_row, above, below = lax.optimization_barrier(
        (parts[half - 1], mask_row, diag_row, above, below)
    )
    parts[half - 1] = last
    trio = jnp.concatenate([above, invs[1], below], axis=0)
    mates = send(trio, lambda r, c: (r, c ^ 1))
    signs = sign_rows(
        parts, slot.astype(jnp.int32)[None], group_order[None], mask_row, diag_row
    )

    def at_step(step, within):
        def target(r, c):
            team, slot = place.work(r, c)
            same = (slot ^ step) // half == c // half
            return (team, slot ^ step) if same or not within else None

        return target

    def onward(step):
        return lambda r, c: (r, c ^ step) if c // half != r % 2 else None

    steps = range(2, half, 2)
    first = [send(signs, at_step(0, False)), send(signs, at_step(half, False))]
    near = [[send(signs, at_step(k ^ j, True)) for j in (0, half)] for k in steps]
    pair, near, mates = lax.optimization_barrier((jnp.concatenate(first, axis=0), near, mates))
    far = [send(pair, onward(k)) for k in steps]
    own = signs.shape[0]
    groups, sources = [[0, half]], [[[(part, 0)] for part in first]]
    groups.append([k ^ j for k in steps for j in (0, half)])
    sources.append(
        [[(near[i][j], 0), (far[i], j)] for i in range(len(near)) for j in range(2)]
    )
    pieces, every, before = [], [], []
    for steps, source in zip(groups, sources):
        out = products(trio, mates, source, own, before)
        beside = [k ^ 1 for k in steps]
        every += steps
        before = [out[0], out[2]]
        pieces += [
            (0, beside, send(out[3], lambda r, c: (r + 1, c ^ 1))),
            (2, beside, send(out[5], lambda r, c: (r - 1, c ^ 1))),
            (1, beside, send(out[4], lambda r, c: (r, c ^ 1))),
            (1, steps, out[1]),
        ]
    pieces.append((0, every, send(before[0], lambda r, c: (r + 1, c))))
    pieces.append((2, every, send(before[1], lambda r, c: (r - 1, c))))
    width = cols * hamiltonian.shape[1]
    result = final(col.astype(jnp.int32)[None], pieces, width)
    return result.transpose(1, 0, 2)


def onsite_of(onsite, place, team, row):
    other = place.send(onsite, lambda r, c: (r ^ 1, c))
    return jnp.where(team == row, onsite, other)


def solution(mesh):
    in_specs = (P("row", "col"), P("row", "col"), P("row"), P(), P(), P(("row", "col"), None, None))
    out_specs = P(("row", "col"), None, None)
    return jax.shard_map(shards, mesh=mesh, in_specs=in_specs, out_specs=out_specs, check_vma=False)
```

```python
import jax
import jax.numpy as jnp
from jax import lax
from jax.experimental import pallas as pl
from jax.experimental.pallas import tpu as pltpu
from jax.sharding import PartitionSpec as P

BLOCK = 32
OWN_BLOCKS = 4
AXES = ("row", "col")
F32 = jnp.float32
BF16 = jnp.bfloat16
LAST = (((1,), (1,)), ((), ()))
LARGEST = 0.09375
CODES = 32766.0
VMEM = pl.BlockSpec(memory_space=pltpu.VMEM)
HBM = pl.BlockSpec(memory_space=pltpu.HBM)
SMEM = pl.BlockSpec(memory_space=pltpu.SMEM)


class Place:
    def __init__(self):
        self.rows = lax.axis_size("row")
        self.cols = lax.axis_size("col")
        self.half = self.cols // 2
        self.devices = [(r, c) for r in range(self.rows) for c in range(self.cols)]

    def work(self, row, col):
        upper = col // self.half
        return (row - row % 2 + upper, col ^ ((row % 2 ^ upper) * self.half))

    def send(self, array, target):
        moves = []
        for row, col in self.devices:
            if target(row, col) is None:
                continue
            to_row, to_col = target(row, col)
            moves.append((row * self.cols + col, to_row % self.rows * self.cols + to_col))
        return lax.ppermute(array, AXES, moves)


def prepare_kernel(pieces, ham_hbm, pattern_hbm, out_hbm, ham, pattern, out, in_sems, out_sems):
    across, blocks = pattern.shape
    height, width = ham.shape
    part = height // pieces
    incoming = [pltpu.make_async_copy(pattern_hbm, pattern, in_sems.at[pieces])]
    outgoing = []
    for p in range(pieces):
        rows = pl.ds(p * part, part)
        incoming.append(pltpu.make_async_copy(ham_hbm.at[rows], ham.at[rows], in_sems.at[p]))
        outgoing.append(pltpu.make_async_copy(out.at[rows], out_hbm.at[rows], out_sems.at[p]))
    for copy in incoming:
        copy.start()
    incoming[0].wait()
    lane = lax.broadcasted_iota(jnp.int32, (across, width), 1) // BLOCK
    spread = (lane == lax.broadcasted_iota(jnp.int32, (across, width), 0)).astype(F32)
    weights = lax.dot_general(
        pattern[...].astype(F32), spread, (((0,), (0,)), ((), ())), preferred_element_type=F32
    )
    for p in range(pieces):
        incoming[p + 1].wait()
        for a in range(p * blocks // pieces, (p + 1) * blocks // pieces):
            rows = slice(a * BLOCK, (a + 1) * BLOCK)
            entry = ham[rows, :] * weights[a : a + 1, :]
            root = jnp.sqrt(jnp.sqrt(jnp.abs(entry) * (1.0 / LARGEST)))
            code = (root * CODES + 0.5).astype(jnp.int32)
            out[rows, :] = jnp.where(entry < 0.0, -code, code).astype(jnp.int16)
        outgoing[p].start()
    for copy in outgoing:
        copy.wait()


def prepare(hamiltonian, pattern):
    pieces = 4
    return pl.pallas_call(
        lambda *refs: prepare_kernel(pieces, *refs),
        out_shape=jax.ShapeDtypeStruct(hamiltonian.shape, jnp.int16),
        in_specs=[HBM, HBM],
        out_specs=HBM,
        scratch_shapes=[
            pltpu.VMEM(hamiltonian.shape, F32),
            pltpu.VMEM(pattern.shape[::-1], jnp.int32),
            pltpu.VMEM(hamiltonian.shape, jnp.int16),
            pltpu.SemaphoreType.DMA((pieces + 1,)),
            pltpu.SemaphoreType.DMA((pieces,)),
        ],
        name="prepare",
    )(hamiltonian, pattern.T)


def sign_kernel(count, slot_ref, active_ref, mask_row, diag_row, *refs):
    shards = refs[:count]
    out_ref, ham, high_ref, low_ref = refs[count:]
    width = ham.shape[0]
    own = out_ref.shape[0]
    slot = slot_ref[0]
    half_scale = 0.5 * LARGEST / CODES**4
    mask_col = jnp.broadcast_to(mask_row[...] * half_scale, (own, width)).T
    for k in range(count):
        start = pl.multiple_of((slot ^ k) * own, own)
        root = shards[k][...].astype(F32)
        entry = (root * jnp.abs(root)) * (root * root)
        ham[:, pl.ds(start, own)] = entry * mask_col * mask_row[:, pl.ds(start, own)]
    rows = lax.broadcasted_iota(jnp.int32, (own, width), 0)
    cols = lax.broadcasted_iota(jnp.int32, (own, width), 1)

    def strip(k, squares):
        at = pl.ds(pl.multiple_of(k * own, own), own)
        diag = jnp.where(cols == rows + k * own, diag_row[...], 0.0)
        both = ham[at, :] + ham[:, at].T + diag
        high = both.astype(BF16)
        high_ref[at, :] = high
        low_ref[at, :] = (both - high.astype(F32)).astype(BF16)
        return squares + jnp.sum(both * both, axis=0, keepdims=True)

    small = count <= 8
    squares = lax.fori_loop(0, count, strip, jnp.zeros((1, width), F32), unroll=small)
    total = jnp.sum(squares, axis=1, keepdims=True)
    active_rows = active_ref[0].astype(F32) * BLOCK
    factor = jnp.sqrt(active_rows / (4.0 * (total + 1e-06)))

    def times(panel):
        high = panel.astype(BF16)
        low = (panel - high.astype(F32)).astype(BF16)
        stacked = jnp.concatenate([high, low], axis=0)
        prod = jnp.dot(stacked, high_ref[...], preferred_element_type=F32)
        rest = jnp.dot(high, low_ref[...], preferred_element_type=F32)
        return factor * (prod[:own] + prod[own:] + rest)

    def cubic(panel):
        return 0.5 * (3.0 * panel - times(times(panel)))

    at = pl.ds(pl.multiple_of(slot * own, own), own)
    first = high_ref[at, :].astype(F32) + low_ref[at, :].astype(F32)
    left = cubic(factor * first)
    inner = lax.fori_loop(0, 2, lambda _, panel: cubic(times(panel)), left, unroll=small)
    out_ref[...] = (0.5 * (3.0 * left - inner)).astype(BF16)


def sign_rows(shards, slot, active, mask_row, diag_row):
    count = len(shards)
    width, own = shards[0].shape
    return pl.pallas_call(
        lambda *refs: sign_kernel(count, *refs),
        out_shape=jax.ShapeDtypeStruct((own, width), BF16),
        in_specs=[SMEM, SMEM] + [VMEM] * (2 + count),
        out_specs=VMEM,
        scratch_shapes=[
            pltpu.VMEM((width, width), F32),
            pltpu.VMEM((width, width), BF16),
            pltpu.VMEM((width, width), BF16),
        ],
        compiler_params=pltpu.CompilerParams(vmem_limit_bytes=6 * 2**20 + 10 * width * width),
        cost_estimate=pl.CostEstimate(
            flops=70 * own * width * width, bytes_accessed=2 * width * width, transcendentals=0
        ),
        name="sign_rows",
    )(slot, active, mask_row[None], diag_row[None], *shards)


def products_kernel(sources, sides, widths, *refs):
    outs = refs[-2 * sides :]
    before = refs[-2 * sides - len(widths) : -2 * sides]
    signs = refs[2 : len(refs) - 2 * sides - len(widths)]
    own = outs[0].shape[0]
    shift = [0] * len(outs)
    for part, side, width in zip(before, (0, 2), widths):
        outs[side][:, :width] = part[...]
        shift[side] = width
    for k, source in enumerate(sources):
        shard = sum(signs[i][j * own : (j + 1) * own, :] for i, j in source)
        for j in range(2):
            prod = lax.dot_general(refs[j][...], shard, LAST, preferred_element_type=F32)
            for side in range(sides):
                out, start = outs[j * sides + side], shift[j * sides + side] + k * own
                block = prod[side * own : (side + 1) * own]
                out[:, start : start + own] = block.astype(out.dtype)


def products(trio, mates, sources, own, before):
    arrays = []
    for source in sources:
        arrays += [a for a, _ in source if all(a is not b for b in arrays)]
    indices = [
        [(next(i for i, b in enumerate(arrays) if b is a), j) for a, j in source]
        for source in sources
    ]
    count, width = len(sources), trio.shape[1]
    sides = trio.shape[0] // own
    shapes = [
        jax.ShapeDtypeStruct((own, count * own), F32 if k == 1 else BF16) for k in range(2 * sides)
    ]
    widths = [part.shape[1] for part in before]
    for part, side in zip(before, (0, 2)):
        shapes[side] = jax.ShapeDtypeStruct((own, count * own + part.shape[1]), BF16)
    return pl.pallas_call(
        lambda *refs: products_kernel(indices, sides, widths, *refs),
        out_shape=shapes,
        in_specs=[VMEM] * (2 + len(arrays) + len(before)),
        out_specs=[VMEM] * (2 * sides),
        compiler_params=pltpu.CompilerParams(vmem_limit_bytes=24 * 2**20),
        cost_estimate=pl.CostEstimate(
            flops=4 * sides * own * width * own * count,
            bytes_accessed=2 * width * own * (2 * sides + count),
            transcendentals=0,
        ),
        name="products",
    )(trio, mates, *arrays, *before)


def final_kernel(places, own, slot_ref, *refs):
    out_hbm, out_ref, sems = refs[-3:]
    copies = []
    for side in (1, 0, 2):
        for part, (at, steps) in zip(refs, places):
            for k, step in enumerate(steps):
                if at == side:
                    start = pl.multiple_of((slot_ref[0] ^ step) * own, own)
                    block = part[:, k * own : (k + 1) * own]
                    out_ref[side, :, pl.ds(start, own)] = block.astype(F32)
        copies.append(pltpu.make_async_copy(out_ref.at[side], out_hbm.at[side], sems.at[side]))
        copies[-1].start()
    for copy in copies:
        copy.wait()


def final(slot, pieces, width):
    places = [(side, steps) for side, steps, _ in pieces]
    flat = [array for _, _, array in pieces]
    own = flat[0].shape[0]
    return pl.pallas_call(
        lambda *refs: final_kernel(places, own, *refs),
        out_shape=jax.ShapeDtypeStruct((3, own, width), F32),
        in_specs=[SMEM] + [VMEM] * len(flat),
        out_specs=HBM,
        scratch_shapes=[pltpu.VMEM((3, own, width), F32), pltpu.SemaphoreType.DMA((3,))],
        compiler_params=pltpu.CompilerParams(vmem_limit_bytes=24 * 2**20),
        cost_estimate=pl.CostEstimate(
            flops=0, bytes_accessed=24 * own * width, transcendentals=0
        ),
        name="final",
    )(slot, *flat)


def shards(hamiltonian, pattern, onsite, members, orders, intersection_inv):
    place = Place()
    cols, half = place.cols, place.half
    row, col = lax.axis_index("row"), lax.axis_index("col")
    team, slot = place.work(row, col)
    team_blocks = cols * OWN_BLOCKS
    send = place.send

    def home(r, c):
        return (r, c) if c // half == r % 2 else (r ^ 1, c ^ half)

    masked = prepare(hamiltonian, pattern)
    held = send(masked, home)
    held, onsite = lax.optimization_barrier((held, onsite))
    parts = [held]
    for step in range(1, half):
        parts.append(send(held, lambda r, c, step=step: (r, c ^ step)))

    invs = intersection_inv.transpose(1, 0, 2)
    above = send(invs[0], lambda r, c: (r - 1, c))
    below = send(invs[2], lambda r, c: (r + 1, c))

    group = team * cols + slot
    group_members = lax.dynamic_index_in_dim(members, group, 0, keepdims=False)
    group_order = lax.dynamic_index_in_dim(orders, group, 0, keepdims=False)
    chosen = (group_members[None, :] == jnp.arange(team_blocks, dtype=jnp.int32)[:, None]) & (
        jnp.arange(members.shape[1])[None, :] < group_order
    )
    mask_row = jnp.repeat(jnp.any(chosen, axis=1).astype(F32), BLOCK)
    diag_row = onsite_of(onsite, place, team, row) * mask_row
    parts += [send(part, lambda r, c: (r ^ 1, c)) for part in parts]
    last, mask_row, diag_row, above, below = lax.optimization_barrier(
        (parts[half - 1], mask_row, diag_row, above, below)
    )
    parts[half - 1] = last
    trio = jnp.concatenate([above, invs[1], below], axis=0)
    mates = send(trio, lambda r, c: (r, c ^ 1))
    signs = sign_rows(
        parts, slot.astype(jnp.int32)[None], group_order[None], mask_row, diag_row
    )

    def at_step(step, within):
        def target(r, c):
            team, slot = place.work(r, c)
            same = (slot ^ step) // half == c // half
            return (team, slot ^ step) if same or not within else None

        return target

    def onward(step):
        return lambda r, c: (r, c ^ step) if c // half != r % 2 else None

    steps = range(2, half, 2)
    first = [send(signs, at_step(0, False)), send(signs, at_step(half, False))]
    near = [[send(signs, at_step(k ^ j, True)) for j in (0, half)] for k in steps]
    pair, near, mates = lax.optimization_barrier((jnp.concatenate(first, axis=0), near, mates))
    far = [send(pair, onward(k)) for k in steps]
    own = signs.shape[0]
    groups, sources = [[0, half]], [[[(part, 0)] for part in first]]
    groups.append([k ^ j for k in steps for j in (0, half)])
    sources.append(
        [[(near[i][j], 0), (far[i], j)] for i in range(len(near)) for j in range(2)]
    )
    pieces, every, before = [], [], []
    for steps, source in zip(groups, sources):
        out = products(trio, mates, source, own, before)
        beside = [k ^ 1 for k in steps]
        every += steps
        before = [out[0], out[2]]
        pieces += [
            (0, beside, send(out[3], lambda r, c: (r + 1, c ^ 1))),
            (2, beside, send(out[5], lambda r, c: (r - 1, c ^ 1))),
            (1, beside, send(out[4], lambda r, c: (r, c ^ 1))),
            (1, steps, out[1]),
        ]
    pieces.append((0, every, send(before[0], lambda r, c: (r + 1, c))))
    pieces.append((2, every, send(before[1], lambda r, c: (r - 1, c))))
    width = cols * hamiltonian.shape[1]
    result = final(col.astype(jnp.int32)[None], pieces, width)
    return result.transpose(1, 0, 2)


def onsite_of(onsite, place, team, row):
    other = place.send(onsite, lambda r, c: (r ^ 1, c))
    return jnp.where(team == row, onsite, other)


def solution(mesh):
    in_specs = (P("row", "col"), P("row", "col"), P("row"), P(), P(), P(("row", "col"), None, None))
    out_specs = P(("row", "col"), None, None)
    return jax.shard_map(shards, mesh=mesh, in_specs=in_specs, out_specs=out_specs, check_vma=False)
```
